32 devices in a mesh: rep: 2 (over x), node: 8 (over z, y), local: 2 (over core).
Axes of the slice: x: 2, y: 2, z: 4, core: 2. Of those that a mesh axis runs over, the one named last changes fastest.
Arguments:
- tokens: bfloat16 [4096, 1024], P(('rep', 'node', 'local')), parts along dimension 0, may hold values from -6 to 6
- grad_out: bfloat16 [4096, 1024], P(('rep', 'node', 'local')), parts along dimension 0, may hold values from -0.59765625 to 0.59765625
- expert_ids: int32 [4096, 8], P(('rep', 'node', 'local')), parts along dimension 0, may hold values from 0 to 31, as said below
- gate_values: bfloat16 [4096, 8], P(('rep', 'node', 'local')), parts along dimension 0, may hold values from 0.049804688 to 1
- w_gate: bfloat16 [32, 1024, 384], P('node', None, 'local'), may hold values from -0.1875 to 0.1875
- w_up: bfloat16 [32, 1024, 384], P('node', None, 'local'), may hold values from -0.1875 to 0.1875
- w_down: bfloat16 [32, 384, 1024], P('node', 'local'), may hold values from -0.3125 to 0.3125
Outputs:
- grad_tokens: bfloat16 [4096, 1024], P(('rep', 'node', 'local')), parts along dimension 0
- grad_gates: float32 [4096, 8], P(('rep', 'node', 'local')), parts along dimension 0
- grad_w_gate: bfloat16 [64, 1024, 384], P(('rep', 'node'), None, 'local'), parts along dimension 0
- grad_w_up: bfloat16 [64, 1024, 384], P(('rep', 'node'), None, 'local'), parts along dimension 0
- grad_w_down: bfloat16 [64, 384, 1024], P(('rep', 'node'), 'local'), parts along dimension 0
The draws below stay inside these ranges and needn't reach their ends.
There are 2 independent parts, one for each index of `rep`. The reference program is written for one: setup_inputs(seed, part) draws one part's arguments, and reference() takes and returns one part's arrays. A program takes and returns all parts, laid end to end along the dimension named above; an argument that names none is the same for every part. Nothing has to cross between parts.
Inputs may be any that keep to these rules, and one draw needn't show every extreme that they name: `expert_ids`: expert e belongs to group e // 4. Each token names 8 different experts lying in exactly 4 different groups, one to three of each. Among the tokens of one device at most 96 reach any one group and at most 192 of their pairs name that group's experts; in the tokens of every device some group is reached by exactly 96 tokens with exactly 192 pairs.
All inputs are finite; a program needn't handle non-finite values.
Results may differ from the reference program's by a relative error of at most 0.0058.
Values may be sent and summed in bfloat16 or wider, within the bound.
A program may use at most 128 MiB of HBM per device.

```python
import math
import jax
import jax.numpy as jnp
from jax import lax

D = 1024
FF = 384
EXP_GRP = 4
LIMIT = 4
TOP = 8
TOK_DEV = 128
TOKENS = 2048
EXPERTS = 32
CAP = 96


def group_block(block_key):
    group_total = EXPERTS // EXP_GRP
    entries = LIMIT * TOK_DEV
    key_extra, key_label, key_token, key_hot, key_order, key_flag, key_pick, key_mix = jax.random.split(block_key, 8)
    labels = jnp.arange(group_total, dtype=jnp.int32)
    hot_group = jax.random.randint(key_hot, (), 0, group_total).astype(jnp.int32)
    remaining = entries - CAP
    base_count = remaining // (group_total - 1)
    leftover = remaining - base_count * (group_total - 1)
    scores = jax.random.permutation(key_extra, group_total).astype(jnp.int32)
    hot_score = jnp.sum(jnp.where(labels == hot_group, scores, 0))
    ranked = scores - (scores > hot_score).astype(jnp.int32)
    extra = ((ranked < leftover) & (labels != hot_group)).astype(jnp.int32)
    counts = jnp.where(labels == hot_group, CAP, base_count + extra).astype(jnp.int32)
    bounds = jnp.cumsum(counts)
    entry_index = jnp.arange(entries, dtype=jnp.int32)
    entry_group = jnp.sum((bounds[None, :] <= entry_index[:, None]).astype(jnp.int32), axis=1)
    relabel = jax.random.permutation(key_label, group_total).astype(jnp.int32)
    entry_group = relabel[entry_group]
    hot_label = relabel[hot_group]
    per_token = entry_group.reshape(LIMIT, TOK_DEV).T
    shuffle = jax.random.permutation(key_token, TOK_DEV)
    per_token = per_token[shuffle]
    is_hot = (per_token == hot_label).astype(jnp.int32)
    order = jax.vmap(lambda part_key: jax.random.permutation(part_key, LIMIT))(jax.random.split(key_order, TOK_DEV)).astype(jnp.int32)
    flags = jax.random.randint(key_flag, (TOK_DEV, LIMIT // 2), 0, 2).astype(jnp.int32)
    column = jnp.arange(LIMIT, dtype=jnp.int32)
    entry_count = jnp.full((TOK_DEV, LIMIT), 2, jnp.int32)
    for pair_index in range(LIMIT // 2):
        raise_mark = (order[:, 2 * pair_index][:, None] == column[None, :]).astype(jnp.int32)
        lower_mark = (order[:, 2 * pair_index + 1][:, None] == column[None, :]).astype(jnp.int32)
        free_pair = (1 - jnp.sum(raise_mark * is_hot, axis=1)) * (1 - jnp.sum(lower_mark * is_hot, axis=1))
        shift = flags[:, pair_index] * free_pair
        entry_count = entry_count + shift[:, None] * (raise_mark - lower_mark)
    picks = jax.vmap(lambda part_key: jax.random.permutation(part_key, EXP_GRP))(jax.random.split(key_pick, TOK_DEV * LIMIT)).astype(jnp.int32)
    picks = picks.reshape(TOK_DEV, LIMIT, EXP_GRP)
    candidates = (per_token[:, :, None] * EXP_GRP + picks).reshape(TOK_DEV, LIMIT * EXP_GRP)
    chosen = (jnp.arange(EXP_GRP, dtype=jnp.int32)[None, None, :] < entry_count[:, :, None]).astype(jnp.int32).reshape(TOK_DEV, LIMIT * EXP_GRP)
    selection = jnp.argsort(1 - chosen, axis=1, stable=True)[:, :TOP].astype(jnp.int32)
    selected = jnp.take_along_axis(candidates, selection, axis=1)
    mixing = jax.vmap(lambda part_key: jax.random.permutation(part_key, TOP))(jax.random.split(key_mix, TOK_DEV)).astype(jnp.int32)
    return jnp.take_along_axis(selected, mixing, axis=1).astype(jnp.int32)


def draw_expert_ids(key, part):
    key = jax.random.fold_in(key, 11)
    block_keys = jax.random.split(key, TOKENS // TOK_DEV)
    return jax.vmap(group_block)(block_keys).reshape(TOKENS, TOP).astype(jnp.int32)


def shard_levels(key, shape, cuts, low, top_value):
    factor_of = 1.0
    for position, shards_of in cuts:
        steps = jax.random.uniform(jax.random.fold_in(jax.random.fold_in(key, 6), position), (shards_of,), jnp.float32, low / len(cuts), top_value / len(cuts))
        factor_of = factor_of * jnp.repeat(jnp.exp(steps), shape[position] // shards_of).reshape((-1,) + (1,) * (len(shape) - 1 - position))
    return factor_of


def centred(key, dims, spread, reach, cuts=(), held_as=jnp.bfloat16):
    array = spread * jax.random.normal(key, dims, jnp.float32)
    if cuts:
        array = array * shard_levels(key, dims, cuts, -0.22, 0.18)
    return jnp.clip(array, -reach, reach).astype(held_as)


def setup_inputs(seed: int = 0, part: int = 0) -> dict:
    keys = jax.random.split(jax.random.key(seed), 8)
    own_keys = jax.random.split(jax.random.fold_in(keys[7], part), 8)
    return {
        "tokens": centred(own_keys[0], (TOKENS, D), 1.0, 6.0, ((0, 16),)),
        "grad_out": centred(own_keys[1], (TOKENS, D), 0.1, 0.59765625, ((0, 16),)),
        "expert_ids": draw_expert_ids(jax.random.fold_in(jax.random.fold_in(keys[7], part), 71), part),
        "gate_values": jnp.clip(jnp.exp(math.log(1.0) - 2.9996462 * jax.random.uniform(own_keys[3], (TOKENS, TOP), jnp.float32) ** shard_levels(own_keys[3], (TOKENS, TOP), ((0, 16),), -0.2, 0.2)), 0.049804688, 1.0).astype(jnp.bfloat16),
        "w_gate": centred(keys[4], (EXPERTS, D, FF), D ** -0.5, 0.1875, ((0, 8), (2, 2))),
        "w_up": centred(keys[5], (EXPERTS, D, FF), D ** -0.5, 0.1875, ((0, 8), (2, 2))),
        "w_down": centred(keys[6], (EXPERTS, FF, D), FF ** -0.5, 0.3125, ((0, 8), (1, 2))),
    }


def silu_terms(pre_gate):
    sigma = jax.nn.sigmoid(pre_gate)
    return pre_gate * sigma, sigma * (1.0 + pre_gate * (1.0 - sigma))


def expert_rows(rows_in, rows_grad, gate_column, gate_weight, up_weight, down_weight):
    pre_gate = jnp.dot(rows_in, gate_weight, preferred_element_type=jnp.float32)
    pre_up = jnp.dot(rows_in, up_weight, preferred_element_type=jnp.float32)
    activated, slope = silu_terms(pre_gate)
    hidden = (activated * pre_up).astype(jnp.bfloat16)
    back_hidden = jnp.dot(rows_grad, down_weight.T, preferred_element_type=jnp.float32)
    gate_grad = jnp.sum(back_hidden * hidden.astype(jnp.float32), axis=1)
    scaled = gate_column[:, None] * back_hidden
    grad_pre_gate = (scaled * pre_up * slope).astype(jnp.bfloat16)
    grad_pre_up = (scaled * activated).astype(jnp.bfloat16)
    input_grad = jnp.dot(grad_pre_gate, gate_weight.T, preferred_element_type=jnp.float32)
    input_grad = input_grad + jnp.dot(grad_pre_up, up_weight.T, preferred_element_type=jnp.float32)
    weighted_grad = (gate_column[:, None] * rows_grad.astype(jnp.float32)).astype(jnp.bfloat16)
    grad_gate_weight = jnp.dot(rows_in.T, grad_pre_gate, preferred_element_type=jnp.float32)
    grad_up_weight = jnp.dot(rows_in.T, grad_pre_up, preferred_element_type=jnp.float32)
    grad_down_weight = jnp.dot(hidden.T, weighted_grad, preferred_element_type=jnp.float32)
    return input_grad, gate_grad, grad_gate_weight, grad_up_weight, grad_down_weight


def reference(tokens, grad_out, expert_ids, gate_values, w_gate, w_up, w_down):
    pair_count = TOKENS * TOP
    flat_expert = expert_ids.reshape(-1).astype(jnp.int32)
    flat_token = (jnp.arange(pair_count, dtype=jnp.int32) // TOP).astype(jnp.int32)
    flat_gate = gate_values.reshape(-1).astype(jnp.float32)
    counts = jax.ops.segment_sum(jnp.ones(pair_count, jnp.int32), flat_expert, num_segments=EXPERTS).astype(jnp.int32)
    padded = ((counts + 127) // 128 * 128).astype(jnp.int32)
    pad_start = (jnp.cumsum(padded) - padded).astype(jnp.int32)
    raw_start = (jnp.cumsum(counts) - counts).astype(jnp.int32)
    ordering = jnp.argsort(flat_expert, stable=True).astype(jnp.int32)
    sorted_expert = flat_expert[ordering]
    rank_inside = (jnp.arange(pair_count, dtype=jnp.int32) - raw_start[sorted_expert]).astype(jnp.int32)
    target = (pad_start[sorted_expert] + rank_inside).astype(jnp.int32)
    block_total = pair_count // 128 + EXPERTS
    slot_token = jnp.zeros(block_total * 128, jnp.int32).at[target].set(flat_token[ordering])
    slot_gate = jnp.zeros(block_total * 128, jnp.float32).at[target].set(flat_gate[ordering])
    slot_pair = jnp.full(block_total * 128, pair_count, jnp.int32).at[target].set(ordering)
    block_first = jnp.arange(block_total, dtype=jnp.int32) * 128
    block_expert = (jnp.sum((pad_start[None, :] <= block_first[:, None]).astype(jnp.int32), axis=1) - 1).astype(jnp.int32)

    def advance(carry, item):
        grad_gate_all, grad_up_all, grad_down_all = carry
        expert, token_index, gate_column = item
        results = expert_rows(tokens[token_index], grad_out[token_index], gate_column, w_gate[expert], w_up[expert], w_down[expert])
        grad_gate_all = grad_gate_all.at[expert].add(results[2])
        grad_up_all = grad_up_all.at[expert].add(results[3])
        grad_down_all = grad_down_all.at[expert].add(results[4])
        return (grad_gate_all, grad_up_all, grad_down_all), (results[0], results[1])

    initial = (jnp.zeros((EXPERTS, D, FF), jnp.float32), jnp.zeros((EXPERTS, D, FF), jnp.float32), jnp.zeros((EXPERTS, FF, D), jnp.float32))
    carry, stacked = lax.scan(advance, initial, (block_expert, slot_token.reshape(block_total, 128), slot_gate.reshape(block_total, 128)))
    input_blocks, gate_blocks = stacked
    grad_tokens = jax.ops.segment_sum(input_blocks.reshape(-1, D), slot_token, num_segments=TOKENS).astype(jnp.bfloat16)
    grad_flat = jnp.zeros(pair_count + 1, jnp.float32).at[slot_pair].set(gate_blocks.reshape(-1))
    grad_gates = grad_flat[:pair_count].reshape(TOKENS, TOP)
    return grad_tokens, grad_gates, carry[0].astype(jnp.bfloat16), carry[1].astype(jnp.bfloat16), carry[2].astype(jnp.bfloat16)
```

```python
import jax
import jax.numpy as jnp
from jax import lax
from jax.experimental import pallas as pl
from jax.experimental.pallas import tpu as pltpu
from jax.sharding import PartitionSpec as P

LIMIT = 4
LANES = 128
BLOCK = 256


def silu_terms(pre_gate):
    sigma = jax.nn.sigmoid(pre_gate)
    return (pre_gate * sigma, sigma * (1.0 + pre_gate * (1.0 - sigma)))


def block_rows(rows_in, rows_grad, gate_column, gate_weight, up_weight, down_weight):
    pre_gate = jnp.dot(rows_in, gate_weight, preferred_element_type=jnp.float32)
    pre_up = jnp.dot(rows_in, up_weight, preferred_element_type=jnp.float32)
    activated, slope = silu_terms(pre_gate)
    hidden = (activated * pre_up).astype(jnp.bfloat16)
    back_hidden = jnp.dot(rows_grad, down_weight.T, preferred_element_type=jnp.float32)
    gate_grad = jnp.sum(back_hidden * hidden.astype(jnp.float32), axis=1)
    scaled = gate_column[:, None] * back_hidden
    grad_pre_gate = (scaled * pre_up * slope).astype(jnp.bfloat16)
    grad_pre_up = (scaled * activated).astype(jnp.bfloat16)
    input_grad = jnp.dot(grad_pre_gate, gate_weight.T, preferred_element_type=jnp.float32)
    input_grad = input_grad + jnp.dot(grad_pre_up, up_weight.T, preferred_element_type=jnp.float32)
    return (input_grad, gate_grad, hidden, grad_pre_gate, grad_pre_up)


def process(rows_in, rows_grad, rows_gate, gate_weights, up_weights, down_weights, pair_bound):
    total_rows, model_width = rows_in.shape
    group_size = rows_gate.shape[1]
    unit_count = gate_weights.shape[2]
    block_limit = (pair_bound + 127 * group_size) // 128
    slot_count = block_limit * 128
    window = min(slot_count, (total_rows + 127) // 128 * 128)
    buffer_rows = slot_count + window
    live = (rows_gate != 0).astype(jnp.int32)
    counts = jnp.sum(live, axis=0)
    padded = (counts + 127) // 128 * 128
    pad_start = jnp.cumsum(padded) - padded
    rank = jnp.cumsum(live, axis=0) - 1
    target = jnp.where(live == 1, pad_start[None, :] + rank, buffer_rows).reshape(-1)
    row_ids = jnp.broadcast_to(
        jnp.arange(total_rows, dtype=jnp.int32)[:, None], live.shape
    ).reshape(-1)
    slot_row = jnp.zeros(buffer_rows, jnp.int32).at[target].set(row_ids, mode="drop")
    slot_gate = (
        jnp.zeros(buffer_rows, jnp.float32)
        .at[target]
        .set(rows_gate.astype(jnp.float32).reshape(-1), mode="drop")
    )
    slot_live = jnp.zeros(buffer_rows, jnp.float32).at[target].set(1.0, mode="drop")
    block_first = jnp.arange(block_limit, dtype=jnp.int32) * 128
    block_expert = (
        jnp.sum((pad_start[None, :] <= block_first[:, None]).astype(jnp.int32), axis=1) - 1
    )
    slot_owner = jnp.concatenate(
        [jnp.repeat(block_expert, 128), jnp.full((window,), -1, jnp.int32)]
    )
    initial = (
        jnp.zeros((total_rows, model_width), jnp.float32),
        jnp.zeros((total_rows, group_size), jnp.float32),
        jnp.zeros((buffer_rows, unit_count), jnp.bfloat16),
        jnp.zeros((buffer_rows, unit_count), jnp.bfloat16),
        jnp.zeros((buffer_rows, unit_count), jnp.bfloat16),
    )

    def advance(index, state):
        input_state, gate_state, hidden_buf, gate_buf, up_buf = state
        first = index * 128
        rows = lax.dynamic_slice_in_dim(slot_row, first, 128, 0)
        gates = lax.dynamic_slice_in_dim(slot_gate, first, 128, 0)
        present = lax.dynamic_slice_in_dim(slot_live, first, 128, 0)
        expert = block_expert[index]
        results = block_rows(
            rows_in[rows],
            rows_grad[rows],
            gates,
            gate_weights[expert],
            up_weights[expert],
            down_weights[expert],
        )
        input_state = input_state.at[rows].add(results[0])
        gate_state = gate_state.at[rows, expert].add(present * results[1])
        hidden_buf = lax.dynamic_update_slice_in_dim(hidden_buf, results[2], first, 0)
        gate_buf = lax.dynamic_update_slice_in_dim(gate_buf, results[3], first, 0)
        up_buf = lax.dynamic_update_slice_in_dim(up_buf, results[4], first, 0)
        return (input_state, gate_state, hidden_buf, gate_buf, up_buf)

    final = lax.fori_loop(0, block_limit, advance, initial)
    hidden_buf, gate_buf, up_buf = (final[2], final[3], final[4])
    gate_list, up_list, down_list = ([], [], [])
    for expert in range(group_size):
        start = pad_start[expert]
        rows = lax.dynamic_slice_in_dim(slot_row, start, window, 0)
        mine = lax.dynamic_slice_in_dim(slot_owner, start, window, 0) == expert
        scale = jnp.where(mine, lax.dynamic_slice_in_dim(slot_gate, start, window, 0), 0.0)
        zero_unit = jnp.zeros((), jnp.bfloat16)
        grad_gate_rows = jnp.where(
            mine[:, None], lax.dynamic_slice_in_dim(gate_buf, start, window, 0), zero_unit
        )
        grad_up_rows = jnp.where(
            mine[:, None], lax.dynamic_slice_in_dim(up_buf, start, window, 0), zero_unit
        )
        hidden_rows = lax.dynamic_slice_in_dim(hidden_buf, start, window, 0)
        inputs = rows_in[rows]
        weighted_grad = (scale[:, None] * rows_grad[rows].astype(jnp.float32)).astype(jnp.bfloat16)
        gate_list.append(jnp.dot(inputs.T, grad_gate_rows, preferred_element_type=jnp.float32))
        up_list.append(jnp.dot(inputs.T, grad_up_rows, preferred_element_type=jnp.float32))
        down_list.append(jnp.dot(hidden_rows.T, weighted_grad, preferred_element_type=jnp.float32))
    return (final[0], final[1], (jnp.stack(gate_list), jnp.stack(up_list), jnp.stack(down_list)))


def routed_on_device(tokens, grad_out, expert_ids, gate_values, w_gate, w_up, w_down):
    token_count, model_width = tokens.shape
    group_size = w_gate.shape[0]
    routed = expert_ids.shape[1]
    node_count = lax.axis_size("node")
    capacity = min(token_count, 3 * LIMIT * token_count // (2 * node_count))
    expert_count = group_size * node_count
    slot_total = node_count * capacity
    pair_bound = node_count * 2 * capacity
    hits = expert_ids[:, :, None] == jnp.arange(expert_count, dtype=jnp.int32)[None, None, :]
    gate_table = jnp.sum(jnp.where(hits, gate_values.astype(jnp.float32)[:, :, None], 0.0), axis=1)
    gate_table = gate_table.reshape(token_count, node_count, group_size)
    reached = jnp.any(
        jnp.any(hits, axis=1).reshape(token_count, node_count, group_size), axis=2
    ).astype(jnp.int32)
    position = jnp.cumsum(reached, axis=0) - 1
    matches = (reached[:, :, None] == 1) & (
        position[:, :, None] == jnp.arange(capacity, dtype=jnp.int32)[None, None, :]
    )
    sources = jnp.sum(
        jnp.where(matches, jnp.arange(token_count, dtype=jnp.int32)[:, None, None], 0), axis=0
    )
    filled = jnp.any(matches, axis=0)
    send_in = tokens[sources]
    send_grad = grad_out[sources]
    picked = gate_table[sources, jnp.arange(node_count, dtype=jnp.int32)[:, None]]
    send_gate = jnp.where(filled[:, :, None], picked, 0.0).astype(jnp.bfloat16)
    recv_in, recv_grad, recv_gate = (
        lax.all_to_all(send_in, "node", split_axis=0, concat_axis=0, tiled=True),
        lax.all_to_all(send_grad, "node", split_axis=0, concat_axis=0, tiled=True),
        lax.all_to_all(send_gate, "node", split_axis=0, concat_axis=0, tiled=True),
    )
    flat_in = recv_in.reshape(slot_total, model_width)
    flat_grad = recv_grad.reshape(slot_total, model_width)
    flat_gate = recv_gate.reshape(slot_total, group_size)
    whole_gate, whole_up, whole_down = (
        lax.all_gather(w_gate, "local", axis=2, tiled=True),
        lax.all_gather(w_up, "local", axis=2, tiled=True),
        lax.all_gather(w_down, "local", axis=1, tiled=True),
    )
    input_grad, gate_grad, weight_grads = process(
        flat_in, flat_grad, flat_gate, whole_gate, whole_up, whole_down, pair_bound
    )
    grad_w_gate, grad_w_up, grad_w_down = (
        lax.psum_scatter(weight_grads[0], "local", scatter_dimension=2, tiled=True),
        lax.psum_scatter(weight_grads[1], "local", scatter_dimension=2, tiled=True),
        lax.psum_scatter(weight_grads[2], "local", scatter_dimension=1, tiled=True),
    )
    back_in, back_gate = (
        lax.all_to_all(
            input_grad.reshape(node_count, capacity, model_width),
            "node",
            split_axis=0,
            concat_axis=0,
            tiled=True,
        ),
        lax.all_to_all(
            gate_grad.reshape(node_count, capacity, group_size),
            "node",
            split_axis=0,
            concat_axis=0,
            tiled=True,
        ),
    )
    owner_group = expert_ids // group_size
    member = expert_ids % group_size
    slot_place = jnp.take_along_axis(position, owner_group, axis=1)
    flat_slot = owner_group * capacity + slot_place
    grad_gates = back_gate.reshape(slot_total, group_size)[flat_slot, member]
    routed_index = jnp.arange(routed, dtype=jnp.int32)
    earlier = (owner_group[:, :, None] == owner_group[:, None, :]) & (
        routed_index[None, None, :] < routed_index[None, :, None]
    )
    first_seen = jnp.logical_not(jnp.any(earlier, axis=2))
    rows_back = back_in.reshape(slot_total, model_width)[flat_slot]
    grad_tokens = jnp.sum(jnp.where(first_seen[:, :, None], rows_back, 0.0), axis=1).astype(
        jnp.bfloat16
    )
    return (
        grad_tokens,
        grad_gates,
        grad_w_gate.astype(jnp.bfloat16),
        grad_w_up.astype(jnp.bfloat16),
        grad_w_down.astype(jnp.bfloat16),
    )


def contract(left, right, left_dim, right_dim):
    return lax.dot_general(
        left, right, (((left_dim,), (right_dim,)), ((), ())), preferred_element_type=jnp.float32
    )


def dense_kernel(
    x_ref,
    g_ref,
    t_ref,
    gate_ref,
    up_ref,
    down_ref,
    pick_ref,
    back_ref,
    dgate_ref,
    dup_ref,
    ddown_ref,
    acc_gate,
    acc_up,
    acc_down,
):
    step = pl.program_id(0)
    width = x_ref.shape[1]
    rows, grads = x_ref[...], g_ref[...]
    pre_gate = contract(rows, gate_ref[...], 1, 1)
    pre_up = contract(rows, up_ref[...], 1, 1)
    back_hidden = contract(grads, down_ref[...], 1, 1)
    gate = contract(t_ref[...], pick_ref[...], 1, 0)
    activated, slope = silu_terms(pre_gate)
    hidden = activated * pre_up
    product = back_hidden * hidden
    high = product.astype(jnp.bfloat16)
    low = (product - high.astype(jnp.float32)).astype(jnp.bfloat16)
    scaled = gate * back_hidden
    grad_gate = (scaled * pre_up * slope).astype(jnp.bfloat16)
    grad_up = (scaled * activated).astype(jnp.bfloat16)
    weighted = (gate * hidden).astype(jnp.bfloat16)
    back_ref[:, :width] = contract(grad_gate, gate_ref[...], 1, 0) + contract(
        grad_up, up_ref[...], 1, 0
    )
    back_ref[:, width:] = contract(high, pick_ref[...], 1, 1) + contract(low, pick_ref[...], 1, 1)
    sums = (
        (acc_gate, dgate_ref, contract(grad_gate, rows, 0, 0)),
        (acc_up, dup_ref, contract(grad_up, rows, 0, 0)),
        (acc_down, ddown_ref, contract(weighted, grads, 0, 0)),
    )

    @pl.when(step == 0)
    def _():
        for acc, _, new in sums:
            acc[...] = new

    @pl.when(step > 0)
    def _():
        for acc, _, new in sums:
            acc[...] += new

    @pl.when(step == pl.num_programs(0) - 1)
    def _():
        for acc, out, _ in sums:
            out[...] = acc[...].astype(jnp.bfloat16)


def dense_rows(payload, gate, up, down, pick):
    total = payload.shape[0]
    units, width = down.shape
    tail = 2 * width // LANES
    whole = lambda shape: pl.BlockSpec(shape, lambda i: (0, 0))
    return pl.pallas_call(
        dense_kernel,
        grid=(total // BLOCK,),
        in_specs=[
            pl.BlockSpec((BLOCK, width), lambda i: (i, 0)),
            pl.BlockSpec((BLOCK, width), lambda i: (i, 1)),
            pl.BlockSpec((BLOCK, LANES), lambda i: (i, tail)),
            whole(down.shape),
            whole(down.shape),
            whole(down.shape),
            whole(pick.shape),
        ],
        out_specs=[
            pl.BlockSpec((BLOCK, width + LANES), lambda i: (i, 0)),
            whole(down.shape),
            whole(down.shape),
            whole(down.shape),
        ],
        out_shape=[
            jax.ShapeDtypeStruct((total, width + LANES), jnp.float32),
            jax.ShapeDtypeStruct(down.shape, jnp.bfloat16),
            jax.ShapeDtypeStruct(down.shape, jnp.bfloat16),
            jax.ShapeDtypeStruct(down.shape, jnp.bfloat16),
        ],
        scratch_shapes=[
            pltpu.VMEM(down.shape, jnp.float32),
            pltpu.VMEM(down.shape, jnp.float32),
            pltpu.VMEM(down.shape, jnp.float32),
        ],
        compiler_params=pltpu.CompilerParams(vmem_limit_bytes=58 * 1024 * 1024),
        cost_estimate=pl.CostEstimate(
            flops=16 * total * width * units,
            bytes_accessed=total * width * 8 + width * units * 12,
            transcendentals=total * units,
        ),
    )(payload, payload, payload, gate, up, down, pick)


def on_device(tokens, grad_out, expert_ids, gate_values, w_gate, w_up, w_down):
    node_count = lax.axis_size("node")
    group_size, width, half = w_gate.shape
    if node_count > 2 * LIMIT or group_size * node_count > LANES:
        return routed_on_device(tokens, grad_out, expert_ids, gate_values, w_gate, w_up, w_down)
    token_count = tokens.shape[0]
    units = group_size * half
    experts = jnp.arange(LANES, dtype=jnp.int32)
    hits = expert_ids[:, :, None] == experts[None, None, :]
    table = jnp.sum(jnp.where(hits, gate_values.astype(jnp.float32)[:, :, None], 0.0), axis=1)
    payload = jnp.concatenate([tokens, grad_out, table.astype(jnp.bfloat16)], axis=1)
    payload = lax.all_gather(payload, ("node", "local"), axis=0, tiled=True)
    gate = w_gate.transpose(0, 2, 1).reshape(units, width)
    up = w_up.transpose(0, 2, 1).reshape(units, width)
    down = w_down.reshape(units, width)
    mine = lax.axis_index("node") * group_size + jnp.arange(units, dtype=jnp.int32) // half
    pick = (experts[:, None] == mine[None, :]).astype(jnp.bfloat16)
    back, grad_gate, grad_up, grad_down = dense_rows(payload, gate, up, down, pick)
    back = lax.psum_scatter(back, ("node", "local"), scatter_dimension=0, tiled=True)
    grad_tokens = back[:, :width].astype(jnp.bfloat16)
    grad_table = back[:, width:]
    grad_gates = jnp.sum(jnp.where(hits, grad_table[:, None, :], 0.0), axis=2)
    return (
        grad_tokens,
        grad_gates,
        grad_gate.reshape(group_size, half, width).transpose(0, 2, 1),
        grad_up.reshape(group_size, half, width).transpose(0, 2, 1),
        grad_down.reshape(group_size, half, width),
    )


def solution(mesh):
    in_specs = (
        P(("rep", "node", "local"), None),
        P(("rep", "node", "local"), None),
        P(("rep", "node", "local"), None),
        P(("rep", "node", "local"), None),
        P("node", None, "local"),
        P("node", None, "local"),
        P("node", "local", None),
    )
    out_specs = (
        P(("rep", "node", "local"), None),
        P(("rep", "node", "local"), None),
        P(("rep", "node"), None, "local"),
        P(("rep", "node"), None, "local"),
        P(("rep", "node"), "local", None),
    )
    return jax.shard_map(
        on_device, mesh=mesh, in_specs=in_specs, out_specs=out_specs, check_vma=False
    )
```

```python
import functools

import jax
import jax.numpy as jnp
from jax import lax
from jax.experimental import pallas as pl
from jax.experimental.pallas import tpu as pltpu
from jax.sharding import PartitionSpec as P

LIMIT = 4
LANES = 128
MESH = pl.DeviceIdType.MESH


def silu_terms(pre_gate):
    sigma = jax.nn.sigmoid(pre_gate)
    return (pre_gate * sigma, sigma * (1.0 + pre_gate * (1.0 - sigma)))


def block_rows(rows_in, rows_grad, gate_column, gate_weight, up_weight, down_weight):
    pre_gate = jnp.dot(rows_in, gate_weight, preferred_element_type=jnp.float32)
    pre_up = jnp.dot(rows_in, up_weight, preferred_element_type=jnp.float32)
    activated, slope = silu_terms(pre_gate)
    hidden = (activated * pre_up).astype(jnp.bfloat16)
    back_hidden = jnp.dot(rows_grad, down_weight.T, preferred_element_type=jnp.float32)
    gate_grad = jnp.sum(back_hidden * hidden.astype(jnp.float32), axis=1)
    scaled = gate_column[:, None] * back_hidden
    grad_pre_gate = (scaled * pre_up * slope).astype(jnp.bfloat16)
    grad_pre_up = (scaled * activated).astype(jnp.bfloat16)
    input_grad = jnp.dot(grad_pre_gate, gate_weight.T, preferred_element_type=jnp.float32)
    input_grad = input_grad + jnp.dot(grad_pre_up, up_weight.T, preferred_element_type=jnp.float32)
    return (input_grad, gate_grad, hidden, grad_pre_gate, grad_pre_up)


def process(rows_in, rows_grad, rows_gate, gate_weights, up_weights, down_weights, pair_bound):
    total_rows, model_width = rows_in.shape
    group_size = rows_gate.shape[1]
    unit_count = gate_weights.shape[2]
    block_limit = (pair_bound + 127 * group_size) // 128
    slot_count = block_limit * 128
    window = min(slot_count, (total_rows + 127) // 128 * 128)
    buffer_rows = slot_count + window
    live = (rows_gate != 0).astype(jnp.int32)
    counts = jnp.sum(live, axis=0)
    padded = (counts + 127) // 128 * 128
    pad_start = jnp.cumsum(padded) - padded
    rank = jnp.cumsum(live, axis=0) - 1
    target = jnp.where(live == 1, pad_start[None, :] + rank, buffer_rows).reshape(-1)
    row_ids = jnp.broadcast_to(
        jnp.arange(total_rows, dtype=jnp.int32)[:, None], live.shape
    ).reshape(-1)
    slot_row = jnp.zeros(buffer_rows, jnp.int32).at[target].set(row_ids, mode="drop")
    slot_gate = (
        jnp.zeros(buffer_rows, jnp.float32)
        .at[target]
        .set(rows_gate.astype(jnp.float32).reshape(-1), mode="drop")
    )
    slot_live = jnp.zeros(buffer_rows, jnp.float32).at[target].set(1.0, mode="drop")
    block_first = jnp.arange(block_limit, dtype=jnp.int32) * 128
    block_expert = (
        jnp.sum((pad_start[None, :] <= block_first[:, None]).astype(jnp.int32), axis=1) - 1
    )
    slot_owner = jnp.concatenate(
        [jnp.repeat(block_expert, 128), jnp.full((window,), -1, jnp.int32)]
    )
    initial = (
        jnp.zeros((total_rows, model_width), jnp.float32),
        jnp.zeros((total_rows, group_size), jnp.float32),
        jnp.zeros((buffer_rows, unit_count), jnp.bfloat16),
        jnp.zeros((buffer_rows, unit_count), jnp.bfloat16),
        jnp.zeros((buffer_rows, unit_count), jnp.bfloat16),
    )

    def advance(index, state):
        input_state, gate_state, hidden_buf, gate_buf, up_buf = state
        first = index * 128
        rows = lax.dynamic_slice_in_dim(slot_row, first, 128, 0)
        gates = lax.dynamic_slice_in_dim(slot_gate, first, 128, 0)
        present = lax.dynamic_slice_in_dim(slot_live, first, 128, 0)
        expert = block_expert[index]
        results = block_rows(
            rows_in[rows],
            rows_grad[rows],
            gates,
            gate_weights[expert],
            up_weights[expert],
            down_weights[expert],
        )
        input_state = input_state.at[rows].add(results[0])
        gate_state = gate_state.at[rows, expert].add(present * results[1])
        hidden_buf = lax.dynamic_update_slice_in_dim(hidden_buf, results[2], first, 0)
        gate_buf = lax.dynamic_update_slice_in_dim(gate_buf, results[3], first, 0)
        up_buf = lax.dynamic_update_slice_in_dim(up_buf, results[4], first, 0)
        return (input_state, gate_state, hidden_buf, gate_buf, up_buf)

    final = lax.fori_loop(0, block_limit, advance, initial)
    hidden_buf, gate_buf, up_buf = (final[2], final[3], final[4])
    gate_list, up_list, down_list = ([], [], [])
    for expert in range(group_size):
        start = pad_start[expert]
        rows = lax.dynamic_slice_in_dim(slot_row, start, window, 0)
        mine = lax.dynamic_slice_in_dim(slot_owner, start, window, 0) == expert
        scale = jnp.where(mine, lax.dynamic_slice_in_dim(slot_gate, start, window, 0), 0.0)
        zero_unit = jnp.zeros((), jnp.bfloat16)
        grad_gate_rows = jnp.where(
            mine[:, None], lax.dynamic_slice_in_dim(gate_buf, start, window, 0), zero_unit
        )
        grad_up_rows = jnp.where(
            mine[:, None], lax.dynamic_slice_in_dim(up_buf, start, window, 0), zero_unit
        )
        hidden_rows = lax.dynamic_slice_in_dim(hidden_buf, start, window, 0)
        inputs = rows_in[rows]
        weighted_grad = (scale[:, None] * rows_grad[rows].astype(jnp.float32)).astype(jnp.bfloat16)
        gate_list.append(jnp.dot(inputs.T, grad_gate_rows, preferred_element_type=jnp.float32))
        up_list.append(jnp.dot(inputs.T, grad_up_rows, preferred_element_type=jnp.float32))
        down_list.append(jnp.dot(hidden_rows.T, weighted_grad, preferred_element_type=jnp.float32))
    return (final[0], final[1], (jnp.stack(gate_list), jnp.stack(up_list), jnp.stack(down_list)))


def routed_on_device(tokens, grad_out, expert_ids, gate_values, w_gate, w_up, w_down):
    token_count, model_width = tokens.shape
    group_size = w_gate.shape[0]
    routed = expert_ids.shape[1]
    node_count = lax.axis_size("node")
    capacity = min(token_count, 3 * LIMIT * token_count // (2 * node_count))
    expert_count = group_size * node_count
    slot_total = node_count * capacity
    pair_bound = node_count * 2 * capacity
    hits = expert_ids[:, :, None] == jnp.arange(expert_count, dtype=jnp.int32)[None, None, :]
    gate_table = jnp.sum(jnp.where(hits, gate_values.astype(jnp.float32)[:, :, None], 0.0), axis=1)
    gate_table = gate_table.reshape(token_count, node_count, group_size)
    reached = jnp.any(
        jnp.any(hits, axis=1).reshape(token_count, node_count, group_size), axis=2
    ).astype(jnp.int32)
    position = jnp.cumsum(reached, axis=0) - 1
    matches = (reached[:, :, None] == 1) & (
        position[:, :, None] == jnp.arange(capacity, dtype=jnp.int32)[None, None, :]
    )
    sources = jnp.sum(
        jnp.where(matches, jnp.arange(token_count, dtype=jnp.int32)[:, None, None], 0), axis=0
    )
    filled = jnp.any(matches, axis=0)
    send_in = tokens[sources]
    send_grad = grad_out[sources]
    picked = gate_table[sources, jnp.arange(node_count, dtype=jnp.int32)[:, None]]
    send_gate = jnp.where(filled[:, :, None], picked, 0.0).astype(jnp.bfloat16)
    recv_in, recv_grad, recv_gate = (
        lax.all_to_all(send_in, "node", split_axis=0, concat_axis=0, tiled=True),
        lax.all_to_all(send_grad, "node", split_axis=0, concat_axis=0, tiled=True),
        lax.all_to_all(send_gate, "node", split_axis=0, concat_axis=0, tiled=True),
    )
    flat_in = recv_in.reshape(slot_total, model_width)
    flat_grad = recv_grad.reshape(slot_total, model_width)
    flat_gate = recv_gate.reshape(slot_total, group_size)
    whole_gate, whole_up, whole_down = (
        lax.all_gather(w_gate, "local", axis=2, tiled=True),
        lax.all_gather(w_up, "local", axis=2, tiled=True),
        lax.all_gather(w_down, "local", axis=1, tiled=True),
    )
    input_grad, gate_grad, weight_grads = process(
        flat_in, flat_grad, flat_gate, whole_gate, whole_up, whole_down, pair_bound
    )
    grad_w_gate, grad_w_up, grad_w_down = (
        lax.psum_scatter(weight_grads[0], "local", scatter_dimension=2, tiled=True),
        lax.psum_scatter(weight_grads[1], "local", scatter_dimension=2, tiled=True),
        lax.psum_scatter(weight_grads[2], "local", scatter_dimension=1, tiled=True),
    )
    back_in, back_gate = (
        lax.all_to_all(
            input_grad.reshape(node_count, capacity, model_width),
            "node",
            split_axis=0,
            concat_axis=0,
            tiled=True,
        ),
        lax.all_to_all(
            gate_grad.reshape(node_count, capacity, group_size),
            "node",
            split_axis=0,
            concat_axis=0,
            tiled=True,
        ),
    )
    owner_group = expert_ids // group_size
    member = expert_ids % group_size
    slot_place = jnp.take_along_axis(position, owner_group, axis=1)
    flat_slot = owner_group * capacity + slot_place
    grad_gates = back_gate.reshape(slot_total, group_size)[flat_slot, member]
    routed_index = jnp.arange(routed, dtype=jnp.int32)
    earlier = (owner_group[:, :, None] == owner_group[:, None, :]) & (
        routed_index[None, None, :] < routed_index[None, :, None]
    )
    first_seen = jnp.logical_not(jnp.any(earlier, axis=2))
    rows_back = back_in.reshape(slot_total, model_width)[flat_slot]
    grad_tokens = jnp.sum(jnp.where(first_seen[:, :, None], rows_back, 0.0), axis=1).astype(
        jnp.bfloat16
    )
    return (
        grad_tokens,
        grad_gates,
        grad_w_gate.astype(jnp.bfloat16),
        grad_w_up.astype(jnp.bfloat16),
        grad_w_down.astype(jnp.bfloat16),
    )


def contract(left, right, left_dim, right_dim):
    return lax.dot_general(
        left, right, (((left_dim,), (right_dim,)), ((), ())), preferred_element_type=jnp.float32
    )


def fused_kernel(
    node_count,
    payload_ref,
    gate_ref,
    up_ref,
    down_ref,
    pick_ref,
    tokens_ref,
    table_ref,
    dgate_ref,
    dup_ref,
    ddown_ref,
    rows_ref,
    acc_gate,
    acc_up,
    acc_down,
    keep,
    share_out,
    share_in,
    back_out,
    back_in,
    row_send,
    row_recv,
    pair_send,
    pair_recv,
    share_send,
    share_recv,
    back_send,
    back_recv,
):
    count = payload_ref.shape[0]
    width = gate_ref.shape[1]
    me = lax.axis_index("node")
    partner = {"local": 1 - lax.axis_index("local")}

    def ahead(s):
        return {"node": lax.rem(me + s, node_count)}

    def behind(s):
        return {"node": lax.rem(me + node_count - s, node_count)}

    def row_copy(s):
        return pltpu.make_async_remote_copy(
            src_ref=payload_ref,
            dst_ref=rows_ref.at[s, pl.ds(0, count)],
            send_sem=row_send.at[s],
            recv_sem=row_recv.at[s],
            device_id=ahead(s),
            device_id_type=MESH,
        )

    def pair_copy(s):
        return pltpu.make_async_remote_copy(
            src_ref=rows_ref.at[s, pl.ds(0, count)],
            dst_ref=rows_ref.at[s, pl.ds(count, count)],
            send_sem=pair_send.at[s],
            recv_sem=pair_recv.at[s],
            device_id=partner,
            device_id_type=MESH,
        )

    def share_copy(s):
        return pltpu.make_async_remote_copy(
            src_ref=share_out.at[s],
            dst_ref=share_in.at[s],
            send_sem=share_send.at[s],
            recv_sem=share_recv.at[s],
            device_id=partner,
            device_id_type=MESH,
        )

    def back_copy(s):
        return pltpu.make_async_remote_copy(
            src_ref=back_out.at[s],
            dst_ref=back_in.at[s],
            send_sem=back_send.at[s],
            recv_sem=back_recv.at[s],
            device_id=behind(s),
            device_id_type=MESH,
        )

    barrier = pltpu.get_barrier_semaphore()
    for s in range(1, node_count):
        pl.semaphore_signal(barrier, inc=1, device_id=ahead(s), device_id_type=MESH)
    pl.semaphore_signal(barrier, inc=1, device_id=partner, device_id_type=MESH)
    pl.semaphore_wait(barrier, node_count)

    for s in range(1, node_count):
        row_copy(s).start()
    rows_ref[0, :count, :] = payload_ref[...]
    pair_copy(0).start()
    for acc in (acc_gate, acc_up, acc_down):
        acc[...] = jnp.zeros_like(acc)

    def finish(s):
        share_copy(s).wait_recv()
        return keep[lax.rem(s, 2)] + share_in[s].astype(jnp.float32)

    def send_back(s):
        back_out[s] = finish(s).astype(jnp.bfloat16)
        back_copy(s).start()

    def advance(s, carry):
        @pl.when(s < node_count - 1)
        def _():
            row_copy(s + 1).wait_recv()
            pair_copy(s + 1).start()

        pair_copy(s).wait_recv()
        rows = rows_ref[s, :, :width]
        grads = rows_ref[s, :, width : 2 * width]
        pre_gate = contract(rows, gate_ref[...], 1, 1)
        pre_up = contract(rows, up_ref[...], 1, 1)
        back_hidden = contract(grads, down_ref[...], 1, 1)
        gate = contract(rows_ref[s, :, 2 * width :], pick_ref[...], 1, 0)
        activated, slope = silu_terms(pre_gate)
        hidden = activated * pre_up
        product = back_hidden * hidden
        high = product.astype(jnp.bfloat16)
        low = (product - high.astype(jnp.float32)).astype(jnp.bfloat16)
        scaled = gate * back_hidden
        grad_gate = (scaled * pre_up * slope).astype(jnp.bfloat16)
        grad_up = (scaled * activated).astype(jnp.bfloat16)
        weighted = (gate * hidden).astype(jnp.bfloat16)
        back = contract(grad_gate, gate_ref[...], 1, 0) + contract(grad_up, up_ref[...], 1, 0)
        sums = contract(high, pick_ref[...], 1, 1) + contract(low, pick_ref[...], 1, 1)
        share_out[s, :, :width] = back[count:].astype(jnp.bfloat16)
        share_out[s, :, width:] = sums[count:].astype(jnp.bfloat16)
        share_copy(s).start()
        keep[lax.rem(s, 2), :, :width] = back[:count]
        keep[lax.rem(s, 2), :, width:] = sums[:count]

        @pl.when(s == 1)
        def _():
            keep[2] = finish(0)

        @pl.when(s > 1)
        def _():
            send_back(s - 1)

        acc_gate[...] += contract(grad_gate, rows, 0, 0)
        acc_up[...] += contract(grad_up, rows, 0, 0)
        acc_down[...] += contract(weighted, grads, 0, 0)
        return carry

    lax.fori_loop(0, node_count, advance, 0)
    send_back(node_count - 1)
    dgate_ref[...] = acc_gate[...].astype(jnp.bfloat16)
    dup_ref[...] = acc_up[...].astype(jnp.bfloat16)
    ddown_ref[...] = acc_down[...].astype(jnp.bfloat16)
    for s in range(1, node_count):
        back_copy(s).wait_recv()
        keep[2] += back_in[s].astype(jnp.float32)
    tokens_ref[...] = keep[2, :, :width].astype(jnp.bfloat16)
    table_ref[...] = keep[2, :, width:]
    for s in range(node_count):
        pair_copy(s).wait_send()
        share_copy(s).wait_send()
        if s > 0:
            row_copy(s).wait_send()
            back_copy(s).wait_send()


def fused(node_count, payload, gate, up, down, pick):
    count = payload.shape[0]
    units, width = down.shape
    wide = width + LANES
    vmem = pl.BlockSpec(memory_space=pltpu.VMEM)
    total = 2 * count * node_count
    return pl.pallas_call(
        functools.partial(fused_kernel, node_count),
        in_specs=[vmem] * 5,
        out_specs=[vmem] * 5,
        out_shape=[
            jax.ShapeDtypeStruct((count, width), jnp.bfloat16),
            jax.ShapeDtypeStruct((count, LANES), jnp.float32),
            jax.ShapeDtypeStruct(down.shape, jnp.bfloat16),
            jax.ShapeDtypeStruct(down.shape, jnp.bfloat16),
            jax.ShapeDtypeStruct(down.shape, jnp.bfloat16),
        ],
        scratch_shapes=[
            pltpu.VMEM((node_count, 2 * count, payload.shape[1]), jnp.bfloat16),
            pltpu.VMEM(down.shape, jnp.float32),
            pltpu.VMEM(down.shape, jnp.float32),
            pltpu.VMEM(down.shape, jnp.float32),
            pltpu.VMEM((3, count, wide), jnp.float32),
        ]
        + [pltpu.VMEM((node_count, count, wide), jnp.bfloat16)] * 4
        + [pltpu.SemaphoreType.DMA((node_count,))] * 8,
        compiler_params=pltpu.CompilerParams(
            collective_id=0, has_side_effects=True, vmem_limit_bytes=60 * 1024 * 1024
        ),
        cost_estimate=pl.CostEstimate(
            flops=16 * total * width * units,
            bytes_accessed=width * units * 12,
            transcendentals=total * units,
        ),
    )(payload, gate, up, down, pick)


def on_device(tokens, grad_out, expert_ids, gate_values, w_gate, w_up, w_down):
    node_count = lax.axis_size("node")
    group_size, width, half = w_gate.shape
    if node_count > 2 * LIMIT or group_size * node_count > LANES:
        return routed_on_device(tokens, grad_out, expert_ids, gate_values, w_gate, w_up, w_down)
    token_count = tokens.shape[0]
    units = group_size * half
    experts = jnp.arange(LANES, dtype=jnp.int32)
    hits = expert_ids[:, :, None] == experts[None, None, :]
    table = jnp.sum(jnp.where(hits, gate_values.astype(jnp.float32)[:, :, None], 0.0), axis=1)
    payload = jnp.concatenate([tokens, grad_out, table.astype(jnp.bfloat16)], axis=1)
    gate = w_gate.transpose(0, 2, 1).reshape(units, width)
    up = w_up.transpose(0, 2, 1).reshape(units, width)
    down = w_down.reshape(units, width)
    mine = lax.axis_index("node") * group_size + jnp.arange(units, dtype=jnp.int32) // half
    pick = (experts[:, None] == mine[None, :]).astype(jnp.bfloat16)
    grad_tokens, grad_table, grad_gate, grad_up, grad_down = fused(
        node_count, payload, gate, up, down, pick
    )
    grad_gates = jnp.sum(jnp.where(hits, grad_table[:, None, :], 0.0), axis=2)
    return (
        grad_tokens,
        grad_gates,
        grad_gate.reshape(group_size, half, width).transpose(0, 2, 1),
        grad_up.reshape(group_size, half, width).transpose(0, 2, 1),
        grad_down.reshape(group_size, half, width),
    )


def solution(mesh):
    in_specs = (
        P(("rep", "node", "local"), None),
        P(("rep", "node", "local"), None),
        P(("rep", "node", "local"), None),
        P(("rep", "node", "local"), None),
        P("node", None, "local"),
        P("node", None, "local"),
        P("node", "local", None),
    )
    out_specs = (
        P(("rep", "node", "local"), None),
        P(("rep", "node", "local"), None),
        P(("rep", "node"), None, "local"),
        P(("rep", "node"), None, "local"),
        P(("rep", "node"), "local", None),
    )
    return jax.shard_map(
        on_device, mesh=mesh, in_specs=in_specs, out_specs=out_specs, check_vma=False
    )
```

```python
import functools

import jax
import jax.numpy as jnp
from jax import lax
from jax.experimental import pallas as pl
from jax.experimental.pallas import tpu as pltpu
from jax.sharding import PartitionSpec as P

LIMIT = 4
LANES = 128
MESH = pl.DeviceIdType.MESH


def silu_terms(pre_gate):
    sigma = jax.nn.sigmoid(pre_gate)
    return (pre_gate * sigma, sigma * (1.0 + pre_gate * (1.0 - sigma)))


def block_rows(rows_in, rows_grad, gate_column, gate_weight, up_weight, down_weight):
    pre_gate = jnp.dot(rows_in, gate_weight, preferred_element_type=jnp.float32)
    pre_up = jnp.dot(rows_in, up_weight, preferred_element_type=jnp.float32)
    activated, slope = silu_terms(pre_gate)
    hidden = (activated * pre_up).astype(jnp.bfloat16)
    back_hidden = jnp.dot(rows_grad, down_weight.T, preferred_element_type=jnp.float32)
    gate_grad = jnp.sum(back_hidden * hidden.astype(jnp.float32), axis=1)
    scaled = gate_column[:, None] * back_hidden
    grad_pre_gate = (scaled * pre_up * slope).astype(jnp.bfloat16)
    grad_pre_up = (scaled * activated).astype(jnp.bfloat16)
    input_grad = jnp.dot(grad_pre_gate, gate_weight.T, preferred_element_type=jnp.float32)
    input_grad = input_grad + jnp.dot(grad_pre_up, up_weight.T, preferred_element_type=jnp.float32)
    return (input_grad, gate_grad, hidden, grad_pre_gate, grad_pre_up)


def process(rows_in, rows_grad, rows_gate, gate_weights, up_weights, down_weights, pair_bound):
    total_rows, model_width = rows_in.shape
    group_size = rows_gate.shape[1]
    unit_count = gate_weights.shape[2]
    block_limit = (pair_bound + 127 * group_size) // 128
    slot_count = block_limit * 128
    window = min(slot_count, (total_rows + 127) // 128 * 128)
    buffer_rows = slot_count + window
    live = (rows_gate != 0).astype(jnp.int32)
    counts = jnp.sum(live, axis=0)
    padded = (counts + 127) // 128 * 128
    pad_start = jnp.cumsum(padded) - padded
    rank = jnp.cumsum(live, axis=0) - 1
    target = jnp.where(live == 1, pad_start[None, :] + rank, buffer_rows).reshape(-1)
    row_ids = jnp.broadcast_to(
        jnp.arange(total_rows, dtype=jnp.int32)[:, None], live.shape
    ).reshape(-1)
    slot_row = jnp.zeros(buffer_rows, jnp.int32).at[target].set(row_ids, mode="drop")
    slot_gate = (
        jnp.zeros(buffer_rows, jnp.float32)
        .at[target]
        .set(rows_gate.astype(jnp.float32).reshape(-1), mode="drop")
    )
    slot_live = jnp.zeros(buffer_rows, jnp.float32).at[target].set(1.0, mode="drop")
    block_first = jnp.arange(block_limit, dtype=jnp.int32) * 128
    block_expert = (
        jnp.sum((pad_start[None, :] <= block_first[:, None]).astype(jnp.int32), axis=1) - 1
    )
    slot_owner = jnp.concatenate(
        [jnp.repeat(block_expert, 128), jnp.full((window,), -1, jnp.int32)]
    )
    initial = (
        jnp.zeros((total_rows, model_width), jnp.float32),
        jnp.zeros((total_rows, group_size), jnp.float32),
        jnp.zeros((buffer_rows, unit_count), jnp.bfloat16),
        jnp.zeros((buffer_rows, unit_count), jnp.bfloat16),
        jnp.zeros((buffer_rows, unit_count), jnp.bfloat16),
    )

    def advance(index, state):
        input_state, gate_state, hidden_buf, gate_buf, up_buf = state
        first = index * 128
        rows = lax.dynamic_slice_in_dim(slot_row, first, 128, 0)
        gates = lax.dynamic_slice_in_dim(slot_gate, first, 128, 0)
        present = lax.dynamic_slice_in_dim(slot_live, first, 128, 0)
        expert = block_expert[index]
        results = block_rows(
            rows_in[rows],
            rows_grad[rows],
            gates,
            gate_weights[expert],
            up_weights[expert],
            down_weights[expert],
        )
        input_state = input_state.at[rows].add(results[0])
        gate_state = gate_state.at[rows, expert].add(present * results[1])
        hidden_buf = lax.dynamic_update_slice_in_dim(hidden_buf, results[2], first, 0)
        gate_buf = lax.dynamic_update_slice_in_dim(gate_buf, results[3], first, 0)
        up_buf = lax.dynamic_update_slice_in_dim(up_buf, results[4], first, 0)
        return (input_state, gate_state, hidden_buf, gate_buf, up_buf)

    final = lax.fori_loop(0, block_limit, advance, initial)
    hidden_buf, gate_buf, up_buf = (final[2], final[3], final[4])
    gate_list, up_list, down_list = ([], [], [])
    for expert in range(group_size):
        start = pad_start[expert]
        rows = lax.dynamic_slice_in_dim(slot_row, start, window, 0)
        mine = lax.dynamic_slice_in_dim(slot_owner, start, window, 0) == expert
        scale = jnp.where(mine, lax.dynamic_slice_in_dim(slot_gate, start, window, 0), 0.0)
        zero_unit = jnp.zeros((), jnp.bfloat16)
        grad_gate_rows = jnp.where(
            mine[:, None], lax.dynamic_slice_in_dim(gate_buf, start, window, 0), zero_unit
        )
        grad_up_rows = jnp.where(
            mine[:, None], lax.dynamic_slice_in_dim(up_buf, start, window, 0), zero_unit
        )
        hidden_rows = lax.dynamic_slice_in_dim(hidden_buf, start, window, 0)
        inputs = rows_in[rows]
        weighted_grad = (scale[:, None] * rows_grad[rows].astype(jnp.float32)).astype(jnp.bfloat16)
        gate_list.append(jnp.dot(inputs.T, grad_gate_rows, preferred_element_type=jnp.float32))
        up_list.append(jnp.dot(inputs.T, grad_up_rows, preferred_element_type=jnp.float32))
        down_list.append(jnp.dot(hidden_rows.T, weighted_grad, preferred_element_type=jnp.float32))
    return (final[0], final[1], (jnp.stack(gate_list), jnp.stack(up_list), jnp.stack(down_list)))


def routed_on_device(tokens, grad_out, expert_ids, gate_values, w_gate, w_up, w_down):
    token_count, model_width = tokens.shape
    group_size = w_gate.shape[0]
    routed = expert_ids.shape[1]
    node_count = lax.axis_size("node")
    capacity = min(token_count, 3 * LIMIT * token_count // (2 * node_count))
    expert_count = group_size * node_count
    slot_total = node_count * capacity
    pair_bound = node_count * 2 * capacity
    hits = expert_ids[:, :, None] == jnp.arange(expert_count, dtype=jnp.int32)[None, None, :]
    gate_table = jnp.sum(jnp.where(hits, gate_values.astype(jnp.float32)[:, :, None], 0.0), axis=1)
    gate_table = gate_table.reshape(token_count, node_count, group_size)
    reached = jnp.any(
        jnp.any(hits, axis=1).reshape(token_count, node_count, group_size), axis=2
    ).astype(jnp.int32)
    position = jnp.cumsum(reached, axis=0) - 1
    matches = (reached[:, :, None] == 1) & (
        position[:, :, None] == jnp.arange(capacity, dtype=jnp.int32)[None, None, :]
    )
    sources = jnp.sum(
        jnp.where(matches, jnp.arange(token_count, dtype=jnp.int32)[:, None, None], 0), axis=0
    )
    filled = jnp.any(matches, axis=0)
    send_in = tokens[sources]
    send_grad = grad_out[sources]
    picked = gate_table[sources, jnp.arange(node_count, dtype=jnp.int32)[:, None]]
    send_gate = jnp.where(filled[:, :, None], picked, 0.0).astype(jnp.bfloat16)
    recv_in, recv_grad, recv_gate = (
        lax.all_to_all(send_in, "node", split_axis=0, concat_axis=0, tiled=True),
        lax.all_to_all(send_grad, "node", split_axis=0, concat_axis=0, tiled=True),
        lax.all_to_all(send_gate, "node", split_axis=0, concat_axis=0, tiled=True),
    )
    flat_in = recv_in.reshape(slot_total, model_width)
    flat_grad = recv_grad.reshape(slot_total, model_width)
    flat_gate = recv_gate.reshape(slot_total, group_size)
    whole_gate, whole_up, whole_down = (
        lax.all_gather(w_gate, "local", axis=2, tiled=True),
        lax.all_gather(w_up, "local", axis=2, tiled=True),
        lax.all_gather(w_down, "local", axis=1, tiled=True),
    )
    input_grad, gate_grad, weight_grads = process(
        flat_in, flat_grad, flat_gate, whole_gate, whole_up, whole_down, pair_bound
    )
    grad_w_gate, grad_w_up, grad_w_down = (
        lax.psum_scatter(weight_grads[0], "local", scatter_dimension=2, tiled=True),
        lax.psum_scatter(weight_grads[1], "local", scatter_dimension=2, tiled=True),
        lax.psum_scatter(weight_grads[2], "local", scatter_dimension=1, tiled=True),
    )
    back_in, back_gate = (
        lax.all_to_all(
            input_grad.reshape(node_count, capacity, model_width),
            "node",
            split_axis=0,
            concat_axis=0,
            tiled=True,
        ),
        lax.all_to_all(
            gate_grad.reshape(node_count, capacity, group_size),
            "node",
            split_axis=0,
            concat_axis=0,
            tiled=True,
        ),
    )
    owner_group = expert_ids // group_size
    member = expert_ids % group_size
    slot_place = jnp.take_along_axis(position, owner_group, axis=1)
    flat_slot = owner_group * capacity + slot_place
    grad_gates = back_gate.reshape(slot_total, group_size)[flat_slot, member]
    routed_index = jnp.arange(routed, dtype=jnp.int32)
    earlier = (owner_group[:, :, None] == owner_group[:, None, :]) & (
        routed_index[None, None, :] < routed_index[None, :, None]
    )
    first_seen = jnp.logical_not(jnp.any(earlier, axis=2))
    rows_back = back_in.reshape(slot_total, model_width)[flat_slot]
    grad_tokens = jnp.sum(jnp.where(first_seen[:, :, None], rows_back, 0.0), axis=1).astype(
        jnp.bfloat16
    )
    return (
        grad_tokens,
        grad_gates,
        grad_w_gate.astype(jnp.bfloat16),
        grad_w_up.astype(jnp.bfloat16),
        grad_w_down.astype(jnp.bfloat16),
    )


def contract(left, right, left_dim, right_dim):
    return lax.dot_general(
        left, right, (((left_dim,), (right_dim,)), ((), ())), preferred_element_type=jnp.float32
    )


def fused_kernel(
    node_count,
    payload_ref,
    gate_ref,
    up_ref,
    down_ref,
    pick_ref,
    tokens_ref,
    table_ref,
    dgate_ref,
    dup_ref,
    ddown_ref,
    rows_ref,
    acc_gate,
    acc_up,
    acc_down,
    keep,
    share_out,
    share_in,
    side_out,
    side_in,
    line_out,
    line_in,
    line_send,
    line_recv,
    side_send,
    side_recv,
    pair_send,
    pair_recv,
    share_send,
    share_recv,
    side_back_send,
    side_back_recv,
    line_back_send,
    line_back_recv,
):
    count = payload_ref.shape[0]
    width = gate_ref.shape[1]
    me = lax.axis_index("node")
    length = node_count // 2
    place, side = me // 2, lax.rem(me, 2)
    partner = {"local": 1 - lax.axis_index("local")}
    across = {"node": 2 * place + 1 - side}

    def ahead(k):
        return {"node": 2 * lax.rem(place + k, length) + side}

    def behind(k):
        return {"node": 2 * lax.rem(place + length - k, length) + side}

    def remote(source, target, send_sem, recv_sem, device):
        return pltpu.make_async_remote_copy(
            src_ref=source,
            dst_ref=target,
            send_sem=send_sem,
            recv_sem=recv_sem,
            device_id=device,
            device_id_type=MESH,
        )

    def line_copy(k):
        target = rows_ref.at[2 * k, pl.ds(0, count)]
        return remote(payload_ref, target, line_send.at[k], line_recv.at[k], ahead(k))

    def side_copy(k):
        source = rows_ref.at[2 * k, pl.ds(0, count)]
        target = rows_ref.at[2 * k + 1, pl.ds(0, count)]
        return remote(source, target, side_send.at[k], side_recv.at[k], across)

    def side_back(k):
        sems = side_back_send.at[k], side_back_recv.at[k]
        return remote(side_out.at[k], side_in.at[k], *sems, across)

    def line_back(k):
        sems = line_back_send.at[k], line_back_recv.at[k]
        return remote(line_out.at[k], line_in.at[k], *sems, behind(k))

    def pair_copy(s):
        return pltpu.make_async_remote_copy(
            src_ref=rows_ref.at[s, pl.ds(0, count)],
            dst_ref=rows_ref.at[s, pl.ds(count, count)],
            send_sem=pair_send.at[s],
            recv_sem=pair_recv.at[s],
            device_id=partner,
            device_id_type=MESH,
        )

    def share_copy(s):
        return pltpu.make_async_remote_copy(
            src_ref=share_out.at[s],
            dst_ref=share_in.at[s],
            send_sem=share_send.at[s],
            recv_sem=share_recv.at[s],
            device_id=partner,
            device_id_type=MESH,
        )

    barrier = pltpu.get_barrier_semaphore()
    for k in range(1, length):
        pl.semaphore_signal(barrier, inc=1, device_id=ahead(k), device_id_type=MESH)
    pl.semaphore_signal(barrier, inc=1, device_id=across, device_id_type=MESH)
    pl.semaphore_signal(barrier, inc=1, device_id=partner, device_id_type=MESH)
    pl.semaphore_wait(barrier, length + 1)

    for k in range(1, length):
        line_copy(k).start()
    rows_ref[0, :count, :] = payload_ref[...]
    side_copy(0).start()
    pair_copy(0).start()
    for acc in (acc_gate, acc_up, acc_down):
        acc[...] = jnp.zeros_like(acc)

    def finish(s):
        share_copy(s).wait_recv()
        k = s // 2
        part = share_in[s].astype(jnp.float32)

        @pl.when(lax.rem(s, 2) == 0)
        def _():
            keep[k] += part

        @pl.when(lax.rem(s, 2) == 1)
        def _():
            side_out[k] = (keep[length] + part).astype(jnp.bfloat16)
            side_back(k).start()

    def send_back(k):
        side_back(k).wait_recv()
        whole = keep[k] + side_in[k].astype(jnp.float32)

        @pl.when(k == 0)
        def _():
            keep[0] = whole

        @pl.when(k > 0)
        def _():
            line_out[k] = whole.astype(jnp.bfloat16)
            line_back(k).start()

    def advance(s, carry):
        k = s // 2
        even = lax.rem(s, 2) == 0
        slot = jnp.where(even, k, length)
        pair_copy(s).wait_recv()
        rows = rows_ref[s, :, :width]
        grads = rows_ref[s, :, width : 2 * width]
        pre_gate = contract(rows, gate_ref[...], 1, 1)
        pre_up = contract(rows, up_ref[...], 1, 1)
        back_hidden = contract(grads, down_ref[...], 1, 1)
        gate = contract(rows_ref[s, :, 2 * width :], pick_ref[...], 1, 0)
        activated, slope = silu_terms(pre_gate)
        hidden = activated * pre_up
        product = back_hidden * hidden
        high = product.astype(jnp.bfloat16)
        low = (product - high.astype(jnp.float32)).astype(jnp.bfloat16)
        scaled = gate * back_hidden
        grad_gate = (scaled * pre_up * slope).astype(jnp.bfloat16)
        grad_up = (scaled * activated).astype(jnp.bfloat16)
        weighted = (gate * hidden).astype(jnp.bfloat16)
        back = contract(grad_gate, gate_ref[...], 1, 0) + contract(grad_up, up_ref[...], 1, 0)
        sums = contract(high, pick_ref[...], 1, 1) + contract(low, pick_ref[...], 1, 1)
        share_out[s, :, :width] = back[count:].astype(jnp.bfloat16)
        share_out[s, :, width:] = sums[count:].astype(jnp.bfloat16)
        share_copy(s).start()

        @pl.when(s > 0)
        def _():
            finish(s - 1)

        keep[slot, :, :width] = back[:count]
        keep[slot, :, width:] = sums[:count]

        @pl.when(even & (k < length - 1))
        def _():
            line_copy(k + 1).wait_recv()
            side_copy(k + 1).start()
            pair_copy(s + 2).start()

        @pl.when(even)
        def _():
            side_copy(k).wait_recv()
            pair_copy(s + 1).start()

        acc_gate[...] += contract(grad_gate, rows, 0, 0)
        acc_up[...] += contract(grad_up, rows, 0, 0)
        acc_down[...] += contract(weighted, grads, 0, 0)

        @pl.when((s > 2) & (lax.rem(s, 2) == 1))
        def _():
            send_back(k - 1)

        return carry

    lax.fori_loop(0, node_count, advance, 0)
    finish(node_count - 1)
    dgate_ref[...] = acc_gate[...].astype(jnp.bfloat16)
    dup_ref[...] = acc_up[...].astype(jnp.bfloat16)
    ddown_ref[...] = acc_down[...].astype(jnp.bfloat16)
    send_back(length - 1)
    for k in range(1, length):
        line_back(k).wait_recv()
        keep[0] += line_in[k].astype(jnp.float32)
    tokens_ref[...] = keep[0, :, :width].astype(jnp.bfloat16)
    table_ref[...] = keep[0, :, width:]
    for s in range(node_count):
        pair_copy(s).wait_send()
        share_copy(s).wait_send()
    for k in range(length):
        side_copy(k).wait_send()
        side_back(k).wait_send()
        if k > 0:
            line_copy(k).wait_send()
            line_back(k).wait_send()


def fused(node_count, payload, gate, up, down, pick):
    count = payload.shape[0]
    units, width = down.shape
    wide = width + LANES
    length = node_count // 2
    vmem = pl.BlockSpec(memory_space=pltpu.VMEM)
    total = 2 * count * node_count
    return pl.pallas_call(
        functools.partial(fused_kernel, node_count),
        in_specs=[vmem] * 5,
        out_specs=[vmem] * 5,
        out_shape=[
            jax.ShapeDtypeStruct((count, width), jnp.bfloat16),
            jax.ShapeDtypeStruct((count, LANES), jnp.float32),
            jax.ShapeDtypeStruct(down.shape, jnp.bfloat16),
            jax.ShapeDtypeStruct(down.shape, jnp.bfloat16),
            jax.ShapeDtypeStruct(down.shape, jnp.bfloat16),
        ],
        scratch_shapes=[
            pltpu.VMEM((node_count, 2 * count, payload.shape[1]), jnp.bfloat16),
            pltpu.VMEM(down.shape, jnp.float32),
            pltpu.VMEM(down.shape, jnp.float32),
            pltpu.VMEM(down.shape, jnp.float32),
            pltpu.VMEM((length + 1, count, wide), jnp.float32),
        ]
        + [pltpu.VMEM((node_count, count, wide), jnp.bfloat16)] * 2
        + [pltpu.VMEM((length, count, wide), jnp.bfloat16)] * 4
        + [pltpu.SemaphoreType.DMA((length,))] * 4
        + [pltpu.SemaphoreType.DMA((node_count,))] * 4
        + [pltpu.SemaphoreType.DMA((length,))] * 4,
        compiler_params=pltpu.CompilerParams(
            collective_id=0, has_side_effects=True, vmem_limit_bytes=60 * 1024 * 1024
        ),
        cost_estimate=pl.CostEstimate(
            flops=16 * total * width * units,
            bytes_accessed=width * units * 12,
            transcendentals=total * units,
        ),
    )(payload, gate, up, down, pick)


def on_device(tokens, grad_out, expert_ids, gate_values, w_gate, w_up, w_down):
    node_count = lax.axis_size("node")
    group_size, width, half = w_gate.shape
    if node_count > 2 * LIMIT or node_count % 2 or group_size * node_count > LANES:
        return routed_on_device(tokens, grad_out, expert_ids, gate_values, w_gate, w_up, w_down)
    token_count = tokens.shape[0]
    units = group_size * half
    experts = jnp.arange(LANES, dtype=jnp.int32)
    hits = expert_ids[:, :, None] == experts[None, None, :]
    table = jnp.sum(jnp.where(hits, gate_values.astype(jnp.float32)[:, :, None], 0.0), axis=1)
    payload = jnp.concatenate([tokens, grad_out, table.astype(jnp.bfloat16)], axis=1)
    gate = w_gate.transpose(0, 2, 1).reshape(units, width)
    up = w_up.transpose(0, 2, 1).reshape(units, width)
    down = w_down.reshape(units, width)
    mine = lax.axis_index("node") * group_size + jnp.arange(units, dtype=jnp.int32) // half
    pick = (experts[:, None] == mine[None, :]).astype(jnp.bfloat16)
    grad_tokens, grad_table, grad_gate, grad_up, grad_down = fused(
        node_count, payload, gate, up, down, pick
    )
    grad_gates = jnp.sum(jnp.where(hits, grad_table[:, None, :], 0.0), axis=2)
    return (
        grad_tokens,
        grad_gates,
        grad_gate.reshape(group_size, half, width).transpose(0, 2, 1),
        grad_up.reshape(group_size, half, width).transpose(0, 2, 1),
        grad_down.reshape(group_size, half, width),
    )


def solution(mesh):
    in_specs = (
        P(("rep", "node", "local"), None),
        P(("rep", "node", "local"), None),
        P(("rep", "node", "local"), None),
        P(("rep", "node", "local"), None),
        P("node", None, "local"),
        P("node", None, "local"),
        P("node", "local", None),
    )
    out_specs = (
        P(("rep", "node", "local"), None),
        P(("rep", "node", "local"), None),
        P(("rep", "node"), None, "local"),
        P(("rep", "node"), None, "local"),
        P(("rep", "node"), "local", None),
    )
    return jax.shard_map(
        on_device, mesh=mesh, in_specs=in_specs, out_specs=out_specs, check_vma=False
    )
```
